32 devices in a mesh: dp: 2 (over y), seq: 16 (over z, x, core).
Axes of the slice: x: 2, y: 2, z: 4, core: 2. Of those that a mesh axis runs over, the one named last changes fastest.
Arguments:
- query_rows: bfloat16 [2, 2560, 1024], P('dp', 'seq'), may hold values from -8 to 8
- key_rows: bfloat16 [2, 2560, 128], P('dp', 'seq'), may hold values from -8 to 8
- value_rows: bfloat16 [2, 2560, 128], P('dp', 'seq'), may hold values from -6 to 6
- out_cotangent: bfloat16 [2, 2560, 1024], P('dp', 'seq'), may hold values from -6 to 6
- turn_lengths: int32 [2, 8], P('dp'), may hold values from 1 to 1280, 2560 in all within a row
- ssm_input: bfloat16 [2, 2560, 256], P('dp', 'seq'), may hold values from -6 to 6
- state_input: bfloat16 [2, 2560, 128], P('dp', 'seq'), may hold values from -0.5 to 0.5
- state_readout: bfloat16 [2, 2560, 128], P('dp', 'seq'), may hold values from -0.5 to 0.5
- log_decay: float32 [2, 4, 2560], P('dp', None, 'seq'), may hold values from -1.2 to 0, as said below
- skip_gain: float32 [4], replicated, may hold values from 0.5 to 1.5
- conv_weight: float32 [4, 256], replicated, may hold values from -3 to 3
- ssm_cotangent: bfloat16 [2, 2560, 256], P('dp', 'seq'), may hold values from -6 to 6
Outputs:
- query_grad: bfloat16 [2, 2560, 1024], P('dp', 'seq')
- key_grad: bfloat16 [2, 2560, 128], P('dp', 'seq')
- value_grad: bfloat16 [2, 2560, 128], P('dp', 'seq')
- input_grad: bfloat16 [2, 2560, 256], P('dp', 'seq')
- state_input_grad: float32 [2, 2560, 128], P('dp', 'seq')
- readout_grad: float32 [2, 2560, 128], P('dp', 'seq')
- decay_grad: float32 [2, 4, 2560], P('dp', None, 'seq')
- skip_grad: float32 [4], replicated
- conv_grad: float32 [4, 256], replicated
The draws below stay inside these ranges and needn't reach their ends.
Inputs may be any that keep to these rules, and one draw needn't show every extreme that they name: `turn_lengths`: each transcript's 8 turn lengths sum to 2560, the longest is exactly 1280. `log_decay`: negative.
All inputs are finite; a program needn't handle non-finite values.
Results may differ from the reference program's by a relative error of at most 0.01.
Values may be sent and summed in bfloat16 or wider, within the bound.
A program may use at most 64 MiB of HBM per device.

```python
import math
import jax
import jax.numpy as jnp
import numpy as np
from jax import lax

TOK_DEV = 160
KVH = 1
QPG = 8
DH = 128
SH = 4
P_SIZE = 64
N = 128
CONV = 4
TURNS = 8
TRANSCRIPT_SPAN = 2560
TRANSCRIPT_COUNT = 2


def draw_query_rows(key, part):
    key = jax.random.fold_in(key, 21)
    shape = (TRANSCRIPT_COUNT, TRANSCRIPT_SPAN, KVH * QPG * DH)
    return jnp.clip(jax.random.normal(key, shape), -4.0, 4.0).astype(jnp.bfloat16)


def draw_key_rows(key, part):
    key = jax.random.fold_in(key, 23)
    shape = (TRANSCRIPT_COUNT, TRANSCRIPT_SPAN, KVH * DH)
    return jnp.clip(jax.random.normal(key, shape), -4.0, 4.0).astype(jnp.bfloat16)


def draw_log_decay(key, part):
    key = jax.random.fold_in(key, 41)
    gentle_random_key, root_random_key, quick_random_key, noise_random_key, spike_random_key = jax.random.split(key, 5)
    share = 0.5
    slow = jax.random.uniform(gentle_random_key, (TRANSCRIPT_COUNT, SH, 1)) < share
    slow_rate = jax.random.uniform(root_random_key, (TRANSCRIPT_COUNT, SH, 1), minval=0.2, maxval=0.8) / TRANSCRIPT_SPAN
    fast_rate = jnp.exp(jax.random.uniform(quick_random_key, (TRANSCRIPT_COUNT, SH, 1), minval=jnp.log(1.0 / 50.0), maxval=jnp.log(1.0 / 30.0)))
    rate = jnp.where(slow, slow_rate, fast_rate)
    rough = jnp.exp(jax.random.uniform(noise_random_key, (TRANSCRIPT_COUNT, SH, TRANSCRIPT_SPAN), minval=-0.4, maxval=0.4))
    marked_positions = jax.random.randint(spike_random_key, (TRANSCRIPT_COUNT, 1, 3), 0, TRANSCRIPT_SPAN)
    hits = jnp.sum((jnp.arange(TRANSCRIPT_SPAN)[None, None, :, None] == marked_positions[:, :, None, :]).astype(jnp.float32), axis=-1)
    return -rate * rough + hits * jnp.log(0.7)


def block_levels(rng, shape, cuts, smallest, top_value):
    gain, own = 1.0, jax.random.fold_in(rng, 6)
    for axis_at, parts in cuts:
        heights = jnp.exp(jax.random.uniform(jax.random.fold_in(own, axis_at), (parts,), jnp.float32, smallest / len(cuts), top_value / len(cuts)))
        gain = gain * jnp.repeat(heights, shape[axis_at] // parts).reshape([-1 if axis == axis_at else 1 for axis in range(len(shape))])
    return gain


def split_up(amount, total, reach, lean):
    loads = [(1 << 20) // math.isqrt(grade ** lean) + 1 for grade in range(2, amount + 1)]
    rest, holding = total - reach - (amount - 1), [1] * (amount - 1)
    while rest > 0:
        movable = [i for i in range(amount - 1) if holding[i] < reach]
        mass, budget = sum([loads[i] for i in movable]), rest
        for i in movable:
            addition = min(reach - holding[i], max(1, budget * loads[i] // mass), rest)
            holding[i] = holding[i] + addition
            rest = rest - addition
    return np.array([reach] + holding)


def ragged(rng, amount, total, bound, skew):
    if amount == 2:
        one = jax.random.randint(rng, (), max(1, total - bound), min(bound, total - 1) + 1)
        return jnp.stack([one, total - one])
    sizes = jnp.asarray(split_up(amount, total, bound, skew), jnp.int32)
    twos = (amount - 1) // 2
    donor, taker = sizes[1:1 + 2 * twos:2], sizes[2:2 + 2 * twos:2]
    margin = jnp.minimum(donor - 1, bound - taker)
    passed = jax.random.randint(jax.random.fold_in(rng, 1), (twos,), 0, 1 << 20) % (margin + 1)
    sizes = sizes.at[1:1 + 2 * twos:2].set(donor - passed).at[2:2 + 2 * twos:2].set(taker + passed)
    return sizes[jax.random.permutation(jax.random.fold_in(rng, 2), amount)]


def gaussian(rng, shape, scale, bound, cuts=(), held_as=jnp.bfloat16):
    values = jax.random.normal(rng, shape, jnp.float32) * scale
    if len(cuts) > 0:
        values = block_levels(rng, shape, cuts, -0.22, 0.18) * values
    return jnp.clip(values, min=-bound, max=bound).astype(held_as)


def setup_inputs(seed: int = 0) -> dict:
    seeds = jax.random.split(jax.random.key(seed), 13)
    return {
        "query_rows": draw_query_rows(jax.random.fold_in(seeds[12], 71), 0),
        "key_rows": draw_key_rows(jax.random.fold_in(seeds[12], 71), 0),
        "value_rows": gaussian(seeds[2], (TRANSCRIPT_COUNT, TRANSCRIPT_SPAN, KVH * DH), 1.0, 6.0, ((0, 2), (1, 16))),
        "out_cotangent": gaussian(seeds[3], (TRANSCRIPT_COUNT, TRANSCRIPT_SPAN, KVH * QPG * DH), 1.0, 6.0, ((0, 2), (1, 16))),
        "turn_lengths": jax.vmap(lambda own: ragged(own, TURNS, TRANSCRIPT_SPAN, TRANSCRIPT_SPAN // 2, 2))(jax.random.split(seeds[4], TRANSCRIPT_COUNT)).reshape((TRANSCRIPT_COUNT, TURNS)).astype(jnp.int32),
        "ssm_input": gaussian(seeds[5], (TRANSCRIPT_COUNT, TRANSCRIPT_SPAN, SH * P_SIZE), 1.0, 6.0, ((0, 2), (1, 16))),
        "state_input": gaussian(seeds[6], (TRANSCRIPT_COUNT, TRANSCRIPT_SPAN, N), N ** -0.5, 0.5, ((0, 2), (1, 16))),
        "state_readout": gaussian(seeds[7], (TRANSCRIPT_COUNT, TRANSCRIPT_SPAN, N), N ** -0.5, 0.5, ((0, 2), (1, 16))),
        "log_decay": draw_log_decay(jax.random.fold_in(seeds[12], 71), 0),
        "skip_gain": jnp.clip(jax.random.uniform(seeds[9], (SH,), jnp.float32, 0.5, 1.5), 0.5, 1.5),
        "conv_weight": gaussian(seeds[10], (CONV, SH * P_SIZE), CONV ** -0.5, 3.0, (), jnp.float32),
        "ssm_cotangent": gaussian(seeds[11], (TRANSCRIPT_COUNT, TRANSCRIPT_SPAN, SH * P_SIZE), 1.0, 6.0, ((0, 2), (1, 16))),
    }


NEG_FILL = -1e+30

def turn_index(turn_lengths, positions):
    bounds = jnp.cumsum(turn_lengths)
    return lax.optimization_barrier(jnp.sum((positions[:, None] >= bounds[None, :]).astype(jnp.int32), axis=1))

def attention_one(pieces):
    query_rows, key_rows, value_rows, out_cotangent, turn_lengths = pieces
    total_rows = query_rows.shape[0]
    positions = jnp.arange(total_rows, dtype=jnp.int32)
    turns = turn_index(turn_lengths, positions)
    allowed = (positions[None, :] <= positions[:, None]) & (turns[None, :] == turns[:, None])
    scale = DH ** (-0.5)
    query = query_rows.reshape(total_rows, KVH, QPG, DH).astype(jnp.float32)
    cotangent = out_cotangent.reshape(total_rows, KVH, QPG, DH).astype(jnp.float32)
    key_vals = key_rows.reshape(total_rows, KVH, DH).astype(jnp.float32)
    value_vals = value_rows.reshape(total_rows, KVH, DH).astype(jnp.float32)
    scores = jnp.einsum('tgqd,sgd->gqts', query, key_vals) * scale
    masked = jnp.where(allowed, scores, NEG_FILL)
    row_top = lax.optimization_barrier(jnp.max(masked, axis=-1))
    row_mass = lax.optimization_barrier(jnp.sum(jnp.where(allowed, jnp.exp(masked - row_top[..., None]), 0.0), axis=-1))
    row_lse = row_top + jnp.log(row_mass)
    prob_f32 = jnp.where(allowed, jnp.exp(scores - row_lse[..., None]), 0.0)
    dprob = jnp.einsum('tgqd,sgd->gqts', cotangent, value_vals)
    row_delta = lax.optimization_barrier(jnp.sum(prob_f32 * dprob, axis=-1))
    prob_bf16 = prob_f32.astype(jnp.bfloat16)
    score_grad = (scale * prob_f32 * (dprob - row_delta[..., None])).astype(jnp.bfloat16)
    score_wide = score_grad.astype(jnp.float32)
    query_grad = jnp.einsum('gqts,sgd->tgqd', score_wide, key_vals)
    key_grad = jnp.einsum('gqts,tgqd->sgd', score_wide, query)
    value_grad = jnp.einsum('gqts,tgqd->sgd', prob_bf16.astype(jnp.float32), cotangent)
    return (query_grad.reshape(total_rows, KVH * QPG * DH).astype(jnp.bfloat16), key_grad.reshape(total_rows, KVH * DH).astype(jnp.bfloat16), value_grad.reshape(total_rows, KVH * DH).astype(jnp.bfloat16))

def ssm_block(state, pieces):
    unit, bmat, cmat, rates = pieces
    local_tok = rates.shape[1]
    cumul = jnp.cumsum(rates, axis=1)
    causal = jnp.arange(local_tok)[:, None] >= jnp.arange(local_tok)[None, :]
    decay = jnp.where(causal[None], jnp.exp(jnp.where(causal[None], cumul[:, :, None] - cumul[:, None, :], 0.0)), 0.0)
    gram_mat = jnp.dot(cmat, bmat.T)
    inside = jnp.einsum('hts,ts,shp->thp', decay, gram_mat, unit)
    carried = jnp.einsum('ht,hpn,tn->thp', jnp.exp(cumul), state, cmat)
    tail_w = jnp.exp(cumul[:, -1:] - cumul)
    new_state = jnp.exp(cumul[:, -1])[:, None, None] * state + jnp.einsum('hs,shp,sn->hpn', tail_w, unit, bmat)
    return (new_state, inside + carried)

def ssm_forward(signal, bmat, cmat, rates, skip_gain, conv_weight):
    total_rows = signal.shape[0]
    padded = jnp.concatenate([jnp.zeros((CONV - 1, signal.shape[1]), jnp.float32), signal], axis=0)
    pre_act = jnp.zeros(signal.shape, jnp.float32)
    for shift_k in range(CONV):
        pre_act = pre_act + conv_weight[shift_k] * padded[CONV - 1 - shift_k:CONV - 1 - shift_k + total_rows]
    unit = jax.nn.silu(pre_act).reshape(total_rows, SH, P_SIZE)
    block_count = total_rows // TOK_DEV
    unit_blocks = unit.reshape(block_count, TOK_DEV, SH, P_SIZE)
    b_blocks = bmat.reshape(block_count, TOK_DEV, N)
    c_blocks = cmat.reshape(block_count, TOK_DEV, N)
    rate_blocks = jnp.transpose(rates.reshape(SH, block_count, TOK_DEV), (1, 0, 2))
    _, outputs = lax.scan(ssm_block, jnp.zeros((SH, P_SIZE, N), jnp.float32), (unit_blocks, b_blocks, c_blocks, rate_blocks))
    direct = unit * skip_gain[None, :, None]
    return (outputs.reshape(total_rows, SH, P_SIZE) + direct).reshape(total_rows, SH * P_SIZE)

def ssm_one(pieces):
    signal, bmat, cmat, rates, skip_gain, conv_weight, cotangent = pieces
    _, pullback = jax.vjp(ssm_forward, signal.astype(jnp.float32), bmat.astype(jnp.float32), cmat.astype(jnp.float32), rates, skip_gain, conv_weight)
    return pullback(cotangent.astype(jnp.float32))

def reference(query_rows, key_rows, value_rows, out_cotangent, turn_lengths, ssm_input, state_input, state_readout, log_decay, skip_gain, conv_weight, ssm_cotangent):
    query_grad, key_grad, value_grad = lax.map(attention_one, (query_rows, key_rows, value_rows, out_cotangent, turn_lengths))
    count = ssm_input.shape[0]
    skips = jnp.broadcast_to(skip_gain, (count,) + skip_gain.shape)
    convs = jnp.broadcast_to(conv_weight, (count,) + conv_weight.shape)
    input_grad, b_grad, c_grad, rate_grad, skip_terms, conv_terms = lax.map(ssm_one, (ssm_input, state_input, state_readout, log_decay, skips, convs, ssm_cotangent))
    return (query_grad, key_grad, value_grad, input_grad.astype(jnp.bfloat16), b_grad, c_grad, rate_grad, lax.optimization_barrier(jnp.sum(skip_terms, axis=0)), lax.optimization_barrier(jnp.sum(conv_terms, axis=0)))
```

```python
from functools import partial

import jax
import jax.numpy as jnp
from jax import lax
from jax.experimental import pallas as pl
from jax.experimental.pallas import tpu as pltpu
from jax.sharding import PartitionSpec as P

QPG = 8
DH = 128
SH = 4
P_SIZE = 64
N = 128
CONV = 4
CH = SH * P_SIZE
LONGEST_TURN = 1280
NEG_FILL = -1e30
CHUNK = 256
MESH = pl.DeviceIdType.MESH
HI = lax.Precision.HIGHEST
F32 = jnp.float32
BF16 = jnp.bfloat16


def dot_nn(a, b, precision=None):
    return lax.dot_general(
        a, b, (((1,), (0,)), ((), ())), precision=precision, preferred_element_type=F32
    )


def dot_nt(a, b, precision=None):
    return lax.dot_general(
        a, b, (((1,), (1,)), ((), ())), precision=precision, preferred_element_type=F32
    )


def split_nn(a, b):
    top = b.astype(BF16)
    return dot_nn(a, top) + dot_nn(a, (b - top.astype(F32)).astype(BF16))


def kernel(
    count,
    dp_count,
    tok,
    window,
    turn_ref,
    skip_ref,
    q_ref,
    k_ref,
    v_ref,
    do_ref,
    x_ref,
    b_ref,
    c_ref,
    rate_ref,
    conv_ref,
    g_ref,
    dq_ref,
    dk_ref,
    dv_ref,
    dx_ref,
    db_ref,
    dc_ref,
    drate_ref,
    tot_ref,
    qs,
    dos,
    kv,
    prob,
    dprob,
    tops,
    mass,
    delta,
    start_row,
    pos_row,
    pb,
    sb,
    dq_acc,
    dkv_own,
    dkv_out,
    dkv_in,
    rates8,
    rim_out,
    rim_in,
    xpad,
    ext,
    head_out,
    head_in,
    scan_out,
    scan_in,
    unit_s,
    act_s,
    mid_out,
    mid_in,
    sums,
    kv_send,
    kv_recv,
    dkv_send,
    dkv_recv,
    scan_send,
    scan_recv,
    mid_send,
    mid_recv,
    rim_sem,
    head_sem,
    sum_send,
    sum_recv,
):
    me = lax.axis_index("seq")
    my_dp = lax.axis_index("dp")
    rows = QPG * tok
    scale = DH ** (-0.5)

    def remote(src, dst, send, recv, to):
        return pltpu.make_async_remote_copy(
            src_ref=src,
            dst_ref=dst,
            send_sem=send,
            recv_sem=recv,
            device_id=(my_dp, to),
            device_id_type=MESH,
        )

    barrier = pltpu.get_barrier_semaphore()

    @pl.loop(1, count)
    def _(k):
        pl.semaphore_signal(
            barrier, inc=1, device_id=(my_dp, lax.rem(me + k, count)), device_id_type=MESH
        )

    @pl.loop(1, dp_count)
    def _(k):
        pl.semaphore_signal(
            barrier, inc=1, device_id=(lax.rem(my_dp + k, dp_count), me), device_id_type=MESH
        )

    kv[0, :, 0:DH] = k_ref[...]
    kv[0, :, DH:] = v_ref[...]
    rim_out[...] = x_ref[tok - 16 :, :]
    for h in range(QPG):
        qs[h * tok : (h + 1) * tok, :] = q_ref[:, h * DH : (h + 1) * DH]
        dos[h * tok : (h + 1) * tok, :] = do_ref[:, h * DH : (h + 1) * DH]
    lane = lax.broadcasted_iota(jnp.int32, (1, rows), 1)
    place = lane
    for h in range(1, QPG):
        place = jnp.where(lane >= h * tok, lane - h * tok, place)
    place = place + me * tok
    pos_row[...] = place
    begin = jnp.zeros((1, rows), jnp.int32)
    bound = jnp.int32(0)
    for j in range(turn_ref.shape[1]):
        bound = bound + turn_ref[0, j]
        begin = jnp.where(place >= bound, bound, begin)
    start_row[...] = begin
    pl.semaphore_wait(barrier, count - 1 + dp_count - 1)

    rim_copy = remote(rim_out, rim_in, rim_sem.at[0], rim_sem.at[1], lax.rem(me + 1, count))

    @pl.when(me + 1 < count)
    def _():
        rim_copy.start()

    def kv_copy(k, to):
        return remote(kv.at[0], kv.at[k], kv_send.at[k], kv_recv.at[k], to)

    @pl.loop(1, window + 1)
    def _(k):
        @pl.when(me + k < count)
        def _():
            kv_copy(k, lax.rem(me + k, count)).start()

    def gather_pass(k, first):
        keys = kv[k, :, 0:DH]
        values = kv[k, :, DH:]
        key_pos = (me - k) * tok + lax.broadcasted_iota(jnp.int32, (tok, CHUNK), 0)
        for c in range(rows // CHUNK):
            cs = slice(c * CHUNK, (c + 1) * CHUNK)
            s = dot_nt(keys, qs[cs, :]) * scale
            ok = key_pos >= start_row[:, cs]
            if first:
                ok = ok & (key_pos <= pos_row[:, cs])
            s = jnp.where(ok, s, NEG_FILL)
            top = jnp.max(s, axis=0, keepdims=True)
            if not first:
                old = tops[0, :, cs]
                top = jnp.maximum(top, old)
            p = jnp.exp(s - top)
            dp = dot_nt(values, dos[cs, :])
            part = jnp.sum(p, axis=0, keepdims=True)
            part_delta = jnp.sum(p * dp, axis=0, keepdims=True)
            if not first:
                f = jnp.exp(old - top)
                part = part + f * mass[:, cs]
                part_delta = part_delta + f * delta[:, cs]
            mass[:, cs] = part
            delta[:, cs] = part_delta
            tops[0, :, cs] = top
            tops[k + 1, :, cs] = top
            prob[k, :, cs] = p
            dprob[k, :, cs] = dp

    gather_pass(0, True)

    @pl.when(me > 0)
    def _():
        rim_copy.wait_recv()

    @pl.when(me == 0)
    def _():
        rim_in[...] = jnp.zeros_like(rim_in)

    rates8[...] = jnp.zeros_like(rates8)
    rates8[0:SH, :] = rate_ref[...]
    xpad[0:16, :] = rim_in[...].astype(F32)
    xpad[16:, :] = x_ref[...].astype(F32)
    pre = conv_ref[0:1, :] * xpad[16 : 16 + tok, :]
    for t in range(1, CONV):
        pre = pre + conv_ref[t : t + 1, :] * xpad[16 - t : 16 - t + tok, :]
    act_s[...] = pre
    unit_s[...] = pre * jax.nn.sigmoid(pre)

    sub_t = lax.broadcasted_iota(jnp.int32, (tok, tok), 0)
    lane_t = lax.broadcasted_iota(jnp.int32, (tok, tok), 1)
    tri_low = (sub_t >= lane_t).astype(F32)
    tri_up = (sub_t <= lane_t).astype(F32)
    head_of = lax.broadcasted_iota(jnp.int32, (8, CH), 1)
    head_id = lax.broadcasted_iota(jnp.int32, (8, CH), 0)
    picks = ((head_of >= head_id * P_SIZE) & (head_of < (head_id + 1) * P_SIZE)).astype(F32)
    cum_col = dot_nt(tri_low, rates8[...], HI)
    cum_row = dot_nn(rates8[...], tri_up, HI)
    cum_wide = dot_nn(cum_col, picks, HI)
    last_wide = cum_wide[tok - 1 : tok, :]
    tail_wide = jnp.exp(last_wide - cum_wide)
    head_wide = jnp.exp(cum_wide)
    gout = g_ref[...]
    b_turned = b_ref[...].astype(F32).T.astype(BF16)
    c_turned = c_ref[...].astype(F32).T.astype(BF16)
    tail_unit = tail_wide * unit_s[...]
    head_gout = head_wide * gout.astype(F32)

    def log_rows(a):
        return jnp.broadcast_to(a, (8, CH))

    for way, (turned, right) in enumerate(((b_turned, tail_unit), (c_turned, head_gout))):
        scan_out[way, 0:N, :] = split_nn(turned, right)
        scan_out[way, N:, :] = log_rows(last_wide)

    def toward(way, k):
        return me + k if way == 0 else me - k

    def inside(i):
        return (i >= 0) & (i < count)

    def scan_copy(way, k):
        return remote(
            scan_out.at[way],
            scan_in.at[way, k - 1],
            scan_send.at[way, k - 1],
            scan_recv.at[way, k - 1],
            lax.rem(toward(way, k) + count, count),
        )

    def mid_copy(way, k):
        return remote(
            mid_out.at[way],
            mid_in.at[way, k - 1],
            mid_send.at[way, k - 1],
            mid_recv.at[way, k - 1],
            lax.rem(toward(way, 4 * k) + count, count),
        )

    mids = -(-count // 4) - 1

    def send_all(make, step, steps):
        for way in range(2):
            for k in range(1, steps + 1):

                @pl.when(inside(toward(way, step * k)))
                def _():
                    make(way, k).start()

    def receive_all(make, into, step, steps):
        for way in range(2):
            for k in range(1, steps + 1):
                here = inside(toward(1 - way, step * k))

                @pl.when(here)
                def _():
                    make(way, k).wait_recv()

                @pl.when(jnp.logical_not(here))
                def _():
                    into[way, k - 1] = jnp.zeros(into.shape[2:], F32)

    def log_of(ref, way, k):
        return ref[way, k - 1, N : N + 1, :]

    send_all(scan_copy, 1, 4)

    def later_blocks(low, high):
        @pl.loop(low, high)
        def _(k):
            @pl.when(me >= k)
            def _():
                kv_copy(k, lax.rem(me + k, count)).wait_recv()
                gather_pass(k, False)

    half = window // 2
    later_blocks(1, half + 1)

    receive_all(scan_copy, scan_in, 1, 4)
    near = []
    for way in range(2):
        total = jnp.zeros((N, CH), F32)
        logs = jnp.zeros((1, CH), F32)
        for k in range(1, 5):
            total = total + jnp.exp(logs) * scan_in[way, k - 1, 0:N, :]
            logs = logs + log_of(scan_in, way, k)
        mid_out[way, 0:N, :] = total
        mid_out[way, N:, :] = log_rows(logs)
        near.append(logs)
    send_all(mid_copy, 4, mids)

    later_blocks(half + 1, window + 1)

    dq_acc[...] = jnp.zeros_like(dq_acc)

    def grad_pass(k):
        for c in range(rows // CHUNK):
            cs = slice(c * CHUNK, (c + 1) * CHUNK)
            inv = 1.0 / mass[:, cs]
            f = jnp.exp(tops[k + 1, :, cs] - tops[0, :, cs]) * inv
            p = prob[k, :, cs] * f
            s = (p * scale) * (dprob[k, :, cs] - delta[:, cs] * inv)
            pb[:, cs] = p.astype(BF16)
            sb[:, cs] = s.astype(BF16)
        keys_turned = kv[k, :, 0:DH].astype(F32).T.astype(BF16)
        dq_acc[...] += dot_nn(keys_turned, sb[...])
        return dot_nn(sb[...], qs[...]), dot_nn(pb[...], dos[...])

    def dkv_copy(k, to):
        return remote(dkv_out.at[k - 1], dkv_in.at[k - 1], dkv_send.at[k], dkv_recv.at[k], to)

    @pl.loop(0, window)
    def _(i):
        k = window - i

        @pl.when(me >= k)
        def _():
            dk, dv = grad_pass(k)
            dkv_out[k - 1, :, 0:DH] = dk.astype(BF16)
            dkv_out[k - 1, :, DH:] = dv.astype(BF16)
            dkv_copy(k, lax.rem(me - k + count, count)).start()

    own_dk, own_dv = grad_pass(0)
    dkv_own[:, 0:DH] = own_dk
    dkv_own[:, DH:] = own_dv
    dq_turned = dq_acc[...].T
    for h in range(QPG):
        dq_ref[:, h * DH : (h + 1) * DH] = dq_turned[h * tok : (h + 1) * tok, :].astype(BF16)

    receive_all(mid_copy, mid_in, 4, mids)
    states = []
    for way in range(2):
        total = mid_out[way, 0:N, :]
        logs = near[way]
        for k in range(1, mids + 1):
            total = total + jnp.exp(logs) * mid_in[way, k - 1, 0:N, :]
            logs = logs + log_of(mid_in, way, k)
        states.append(total)
    entry, leaving = states
    entry_b, leaving_b = entry.astype(BF16), leaving.astype(BF16)

    bmat, cmat = b_ref[...], c_ref[...]
    unit = unit_s[...]
    gout_wide = gout.astype(F32)
    pulled = tail_wide * split_nn(bmat, leaving)
    readout = head_wide * split_nn(cmat, entry)
    gram = dot_nt(bmat, cmat)
    lane_c = lax.broadcasted_iota(jnp.int32, (1, CH), 1)
    skip_wide = jnp.zeros((1, CH), F32)
    unit_grad = pulled
    gram_grad = jnp.zeros((tok, tok), F32)
    ones8 = jnp.ones((8, tok), F32)
    row8 = lax.broadcasted_iota(jnp.int32, (8, tok), 0)
    flow = jnp.zeros((8, tok), F32)
    for h in range(SH):
        mine = (lane_c >= h * P_SIZE) & (lane_c < (h + 1) * P_SIZE)
        skip_wide = jnp.where(mine, skip_ref[h], skip_wide)
        gap = jnp.minimum(cum_row[h : h + 1, :] - cum_col[:, h : h + 1], 0.0)
        decay = jnp.where(lane_t >= sub_t, jnp.exp(gap), 0.0)
        mixed = gram * decay
        unit_h = jnp.where(mine, unit, 0.0)
        unit_top = unit_h.astype(BF16)
        unit_rest = (unit_h - unit_top.astype(F32)).astype(BF16)
        gout_h = jnp.where(mine, gout_wide, 0.0).astype(BF16)
        unit_grad = unit_grad + dot_nn(mixed.astype(BF16), gout_h)
        outer = dot_nt(unit_top, gout) + dot_nt(unit_rest, gout)
        gram_grad = gram_grad + outer * decay
        direct = outer * mixed
        flow_h = jnp.sum(direct, axis=0, keepdims=True) - dot_nt(ones8, direct, HI)
        flow = jnp.where(row8 == h, flow_h, flow)
    unit_grad = unit_grad + skip_wide * gout_wide
    pre = act_s[...]
    sig = jax.nn.sigmoid(pre)
    pre_grad = unit_grad * sig * (1.0 + pre * (1.0 - sig))
    ext[0:tok, :] = pre_grad
    head_out[...] = ext[0:8, :]
    head_copy = remote(
        head_out, head_in, head_sem.at[0], head_sem.at[1], lax.rem(me + count - 1, count)
    )

    @pl.when(me > 0)
    def _():
        head_copy.start()

    sum_row = lax.broadcasted_iota(jnp.int32, (8, CH), 0)
    local = jnp.zeros((8, CH), F32)
    for t in range(CONV):
        term = jnp.sum(pre_grad * xpad[16 - t : 16 - t + tok, :], axis=0, keepdims=True)
        local = jnp.where(sum_row == t, term, local)
    local = jnp.where(sum_row == CONV, jnp.sum(gout_wide * unit, axis=0, keepdims=True), local)

    line, column = me // 4, me % 4
    groups = (
        (count // 4, line, lambda j: (my_dp, j * 4 + column)),
        (4, column, lambda j: (my_dp, line * 4 + j)),
        (dp_count, my_dp, lambda j: (j, me)),
    )

    def sum_copy(g, own, j, to, slot):
        return pltpu.make_async_remote_copy(
            src_ref=sums.at[g, own],
            dst_ref=sums.at[g, slot],
            send_sem=sum_send.at[g, j],
            recv_sem=sum_recv.at[g, slot],
            device_id=to,
            device_id_type=MESH,
        )

    def sum_start(g, value):
        size, own, where = groups[g]
        sums[g, own] = value
        for j in range(size):

            @pl.when(own != j)
            def _():
                sum_copy(g, own, j, where(j), own).start()

    def sum_finish(g):
        size, own, where = groups[g]
        for j in range(size):

            @pl.when(own != j)
            def _():
                copy = sum_copy(g, own, j, where(j), j)
                copy.wait_send()
                copy.wait_recv()

        value = sums[g, 0]
        for j in range(1, size):
            value = value + sums[g, j]
        return value

    sum_start(0, local)
    gram_grad_b = gram_grad.astype(BF16)
    db_ref[...] = dot_nn(gram_grad_b, cmat) + dot_nt(tail_unit.astype(BF16), leaving_b)
    gram_turned = gram_grad.T.astype(BF16)
    dc_ref[...] = dot_nn(gram_turned, bmat) + dot_nt(head_gout.astype(BF16), entry_b)
    sum_start(1, sum_finish(0))
    flow = flow + dot_nt(picks, gout_wide * readout, HI)
    kept = dot_nt(picks, unit * pulled, HI)
    ends = jnp.exp(last_wide) * jnp.sum(leaving * entry, axis=0, keepdims=True)
    end = dot_nt(picks, jnp.broadcast_to(ends, (8, CH)), HI)
    strict_up = (sub_t < lane_t).astype(F32)
    drate = dot_nn(flow, tri_low, HI) + dot_nn(kept, strict_up, HI) + end[:, 0:1]
    drate_ref[...] = drate[0:SH, :]
    sum_start(2, sum_finish(1))

    @pl.when(me + 1 < count)
    def _():
        head_copy.wait_recv()

    @pl.when(me + 1 == count)
    def _():
        head_in[...] = jnp.zeros_like(head_in)

    ext[tok:, :] = head_in[...]
    dx = conv_ref[0:1, :] * ext[0:tok, :]
    for t in range(1, CONV):
        dx = dx + conv_ref[t : t + 1, :] * ext[t : t + tok, :]
    dx_ref[...] = dx.astype(BF16)
    tot_ref[...] = sum_finish(2)

    @pl.loop(1, window + 1)
    def _(k):
        @pl.when(me + k < count)
        def _():
            dkv_copy(k, lax.rem(me + k, count)).wait_recv()
            dkv_own[...] += dkv_in[k - 1].astype(F32)
            kv_copy(k, lax.rem(me + k, count)).wait_send()

        @pl.when(me >= k)
        def _():
            dkv_copy(k, lax.rem(me - k + count, count)).wait_send()

    dk_ref[...] = dkv_own[:, 0:DH].astype(BF16)
    dv_ref[...] = dkv_own[:, DH:].astype(BF16)

    @pl.when(me + 1 < count)
    def _():
        rim_copy.wait_send()

    @pl.when(me > 0)
    def _():
        head_copy.wait_send()

    for make, step, steps in ((scan_copy, 1, 4), (mid_copy, 4, mids)):
        for way in range(2):
            for k in range(1, steps + 1):

                @pl.when(inside(toward(way, step * k)))
                def _():
                    make(way, k).wait_send()


def local(
    count,
    dp_count,
    query_rows,
    key_rows,
    value_rows,
    out_cotangent,
    turn_lengths,
    ssm_input,
    state_input,
    state_readout,
    log_decay,
    skip_gain,
    conv_weight,
    ssm_cotangent,
):
    tok = query_rows.shape[1]
    rows = QPG * tok
    window = min(count - 1, -(-(LONGEST_TURN - 1) // tok))
    slots = window + 1
    mids = -(-count // 4) - 1
    span = max(count // 4, 4, dp_count)
    vmem = pl.BlockSpec(memory_space=pltpu.VMEM)
    smem = pl.BlockSpec(memory_space=pltpu.SMEM)
    dma = pltpu.SemaphoreType.DMA
    outs = pl.pallas_call(
        partial(kernel, count, dp_count, tok, window),
        out_shape=(
            jax.ShapeDtypeStruct((tok, QPG * DH), BF16),
            jax.ShapeDtypeStruct((tok, DH), BF16),
            jax.ShapeDtypeStruct((tok, DH), BF16),
            jax.ShapeDtypeStruct((tok, CH), BF16),
            jax.ShapeDtypeStruct((tok, N), F32),
            jax.ShapeDtypeStruct((tok, N), F32),
            jax.ShapeDtypeStruct((SH, tok), F32),
            jax.ShapeDtypeStruct((8, CH), F32),
        ),
        in_specs=[smem, smem] + [vmem] * 10,
        out_specs=(vmem,) * 8,
        scratch_shapes=[
            pltpu.VMEM((rows, DH), BF16),
            pltpu.VMEM((rows, DH), BF16),
            pltpu.VMEM((slots, tok, 2 * DH), BF16),
            pltpu.VMEM((slots, tok, rows), F32),
            pltpu.VMEM((slots, tok, rows), F32),
            pltpu.VMEM((slots + 1, 1, rows), F32),
            pltpu.VMEM((1, rows), F32),
            pltpu.VMEM((1, rows), F32),
            pltpu.VMEM((1, rows), jnp.int32),
            pltpu.VMEM((1, rows), jnp.int32),
            pltpu.VMEM((tok, rows), BF16),
            pltpu.VMEM((tok, rows), BF16),
            pltpu.VMEM((DH, rows), F32),
            pltpu.VMEM((tok, 2 * DH), F32),
            pltpu.VMEM((window, tok, 2 * DH), BF16),
            pltpu.VMEM((window, tok, 2 * DH), BF16),
            pltpu.VMEM((8, tok), F32),
            pltpu.VMEM((16, CH), BF16),
            pltpu.VMEM((16, CH), BF16),
            pltpu.VMEM((16 + tok, CH), F32),
            pltpu.VMEM((tok + 8, CH), F32),
            pltpu.VMEM((8, CH), F32),
            pltpu.VMEM((8, CH), F32),
            pltpu.VMEM((2, N + 8, CH), F32),
            pltpu.VMEM((2, 4, N + 8, CH), F32),
            pltpu.VMEM((tok, CH), F32),
            pltpu.VMEM((tok, CH), F32),
            pltpu.VMEM((2, N + 8, CH), F32),
            pltpu.VMEM((2, mids, N + 8, CH), F32),
            pltpu.VMEM((3, span, 8, CH), F32),
            dma((slots,)),
            dma((slots,)),
            dma((slots,)),
            dma((slots,)),
            dma((2, 4)),
            dma((2, 4)),
            dma((2, mids)),
            dma((2, mids)),
            dma((2,)),
            dma((2,)),
            dma((3, span)),
            dma((3, span)),
        ],
        compiler_params=pltpu.CompilerParams(
            collective_id=0, has_side_effects=True, vmem_limit_bytes=48 * 1024 * 1024
        ),
    )(
        turn_lengths,
        skip_gain,
        query_rows[0],
        key_rows[0],
        value_rows[0],
        out_cotangent[0],
        ssm_input[0],
        state_input[0],
        state_readout[0],
        log_decay[0],
        conv_weight,
        ssm_cotangent[0],
    )
    dq, dk, dv, dx, db, dc, drate, totals = outs
    skip = jnp.sum(totals[CONV].reshape(SH, P_SIZE), axis=1)
    return (dq[None], dk[None], dv[None], dx[None], db[None], dc[None], drate[None], skip, totals[:CONV])


def solution(mesh):
    row = P("dp", "seq", None)
    in_specs = (row, row, row, row, P("dp", None), row, row, row, P("dp", None, "seq"), P(), P(), row)
    out_specs = (row, row, row, row, row, row, P("dp", None, "seq"), P(), P())
    return jax.shard_map(
        partial(local, mesh.shape["seq"], mesh.shape["dp"]),
        mesh=mesh,
        in_specs=in_specs,
        out_specs=out_specs,
        check_vma=False,
    )
```
